32 devices in a mesh: replica: 4 (over y, x), group: 8 (over z, core).
Axes of the slice: x: 2, y: 2, z: 4, core: 2. Of those that a mesh axis runs over, the one named last changes fastest.
Arguments:
- tokens: bfloat16 [64, 512, 768], P(('replica', 'group')), may hold values from -6 to 6
- lengths: int32 [64], replicated, may hold values from 1 to 512, as said below
- slot_order: int32 [64], P(('replica', 'group')), may hold values from 0 to 63, each once
- qkv_weight: bfloat16 [768, 2304], P('replica'), may hold values from -0.21875 to 0.21875
- qv_bias: bfloat16 [1536], P('replica'), may hold values from -3 to 3
- out_weight: bfloat16 [768, 768], P('replica'), may hold values from -2.5 to 2.5
- out_bias: bfloat16 [768], P('replica'), may hold values from -3 to 3
- attn_gain: bfloat16 [768], P('replica'), may hold values from 0.25 to 1.75
- attn_shift: bfloat16 [768], P('replica'), may hold values from -3 to 3
- up_weight: bfloat16 [768, 3072], P('replica'), may hold values from -0.21875 to 0.21875
- up_bias: bfloat16 [3072], P('replica'), may hold values from -3 to 3
- down_weight: bfloat16 [3072, 768], P('replica'), may hold values from -0.109375 to 0.109375
- down_bias: bfloat16 [768], P('replica'), may hold values from -3 to 3
- mlp_gain: bfloat16 [768], P('replica'), may hold values from 0.25 to 1.75
- mlp_shift: bfloat16 [768], P('replica'), may hold values from -3 to 3
- cotangent: bfloat16 [64, 512, 768], P(('replica', 'group')), may hold values from -6 to 6
Outputs:
- layer_out: bfloat16 [64, 512, 768], P(('replica', 'group'))
- grad_tokens: bfloat16 [64, 512, 768], P(('replica', 'group'))
- grad_qkv_weight: float32 [768, 2304], P('replica')
- grad_qv_bias: float32 [1536], P('replica')
- grad_out_weight: float32 [768, 768], P('replica')
- grad_out_bias: float32 [768], P('replica')
- grad_attn_gain: float32 [768], P('replica')
- grad_attn_shift: float32 [768], P('replica')
- grad_up_weight: float32 [768, 3072], P('replica')
- grad_up_bias: float32 [3072], P('replica')
- grad_down_weight: float32 [3072, 768], P('replica')
- grad_down_bias: float32 [768], P('replica')
- grad_mlp_gain: float32 [768], P('replica')
- grad_mlp_shift: float32 [768], P('replica')
The draws below stay inside these ranges and needn't reach their ends.
Inputs may be any that keep to these rules, and one draw needn't show every extreme that they name: `lengths`: some sequence has exactly 512 tokens and some has exactly 1. `slot_order`: A permutation of the 64 sequences over the slots.
All inputs are finite; a program needn't handle non-finite values.
Results may differ from the reference program's by a relative error of at most 0.02.
Values may be sent and summed in bfloat16 or wider, within the bound.
A program may use at most 192 MiB of HBM per device.

```python
from functools import partial
import jax
import jax.numpy as jnp
from jax import lax

D = 768
HEADS = 12
HD = 64
FF = 3072
SEQ = 512
NSEQ = 64


def draw_lengths(key, part):
    key = jax.random.fold_in(key, 5)
    first, second, third, fourth = jax.random.split(key, 4)
    longer = jnp.maximum(jax.random.randint(first, (NSEQ,), 1, SEQ + 1), jax.random.randint(second, (NSEQ,), 1, SEQ + 1))
    chosen = jax.random.randint(third, (), 0, NSEQ)
    other = (chosen + jax.random.randint(fourth, (), 1, NSEQ)) % NSEQ
    places = jnp.arange(NSEQ)
    longer = jnp.where(places == chosen, SEQ, longer)
    longer = jnp.where(places == other, 1, longer)
    return longer.astype(jnp.int32)


def shard_levels(rng, extent, cuts, smallest, top_value):
    loudness, own = 1.0, jax.random.fold_in(rng, 6)
    for position, shards_of in cuts:
        draws = jnp.exp(jax.random.uniform(jax.random.fold_in(own, position), (shards_of,), jnp.float32, smallest / len(cuts), top_value / len(cuts)))
        loudness = loudness * jnp.repeat(draws, extent[position] // shards_of).reshape([-1 if axis == position else 1 for axis in range(len(extent))])
    return loudness


def noise(key, extent, deviation, most, shards=(), kind=jnp.bfloat16):
    gain = shard_levels(key, extent, shards, -0.22, 0.18) if shards else 1.0
    entries = jax.random.normal(key, extent, jnp.float32) * deviation * gain
    return jnp.minimum(jnp.maximum(entries, -most), most).astype(kind)


def setup_inputs(seed: int = 0) -> dict:
    streams_of = jax.random.split(jax.random.key(seed), 17)
    return {
        "tokens": noise(streams_of[0], (NSEQ, SEQ, D), 1.0, 6.0, ((0, 32),)),
        "lengths": draw_lengths(jax.random.fold_in(streams_of[16], 71), 0),
        "slot_order": jax.random.permutation(streams_of[2], NSEQ).astype(jnp.int32),
        "qkv_weight": noise(streams_of[3], (D, 3 * D), D ** -0.5, 0.21875, ((0, 4),)),
        "qv_bias": noise(streams_of[4], (2 * D,), 0.5, 3.0, ((0, 4),)),
        "out_weight": noise(streams_of[5], (D, D), (max(4 * D // SEQ, 1)) ** -0.5, 2.5, ((0, 4),)),
        "out_bias": noise(streams_of[6], (D,), 0.5, 3.0, ((0, 4),)),
        "attn_gain": jnp.clip(1.0 + 0.15 * jax.random.normal(streams_of[7], (D,), jnp.float32), 0.25, 1.75).astype(jnp.bfloat16),
        "attn_shift": noise(streams_of[8], (D,), 0.5, 3.0, ((0, 4),)),
        "up_weight": noise(streams_of[9], (D, FF), D ** -0.5, 0.21875, ((0, 4),)),
        "up_bias": noise(streams_of[10], (FF,), 0.5, 3.0, ((0, 4),)),
        "down_weight": noise(streams_of[11], (FF, D), FF ** -0.5, 0.109375, ((0, 4),)),
        "down_bias": noise(streams_of[12], (D,), 0.5, 3.0, ((0, 4),)),
        "mlp_gain": jnp.clip(1.0 + 0.15 * jax.random.normal(streams_of[13], (D,), jnp.float32), 0.25, 1.75).astype(jnp.bfloat16),
        "mlp_shift": noise(streams_of[14], (D,), 0.5, 3.0, ((0, 4),)),
        "cotangent": noise(streams_of[15], (NSEQ, SEQ, D), 1.0, 6.0, ((0, 32),)),
    }


@jax.custom_vjp
def low(v):
    return lax.optimization_barrier(v.astype(jnp.bfloat16)).astype(jnp.float32)

@jax.custom_vjp
def low_back(v):
    return v

def low_keep(v):
    return (low(v), None)

def low_pass(kept, grad):
    return (grad,)

def back_keep(v):
    return (v, None)

def back_low(kept, grad):
    return (low(grad),)
low.defvjp(low_keep, low_pass)
low_back.defvjp(back_keep, back_low)

def layer_norm(row_data, gain_row, shift_row):
    row_mean = lax.optimization_barrier(jnp.mean(row_data, axis=-1, keepdims=True))
    centred = row_data - row_mean
    spread = lax.optimization_barrier(jnp.mean(centred * centred, axis=-1, keepdims=True))
    return centred * lax.rsqrt(spread + 1e-06) * gain_row + shift_row

def gelu_exact(values):
    return 0.5 * values * (1.0 + lax.erf(values * 0.7071067811865476))

def mixed(form, left, right):
    return jnp.einsum(form, left, right, precision=lax.Precision.HIGHEST)

def block_forward(params, row_data, slot_lens):
    qkv_weight, qv_bias, out_weight, out_bias, attn_gain, attn_shift, up_weight, up_bias, down_weight, down_bias, mlp_gain, mlp_shift = params
    batch = row_data.shape[0]
    key_zero = jnp.zeros((D,), jnp.float32)
    bias_row = jnp.concatenate([qv_bias[:D], key_zero, qv_bias[D:]])
    projected = low(low_back(mixed('bsd,de->bse', row_data, qkv_weight) + bias_row))
    split = projected.reshape(batch, SEQ, 3, HEADS, HD)
    queries = split[:, :, 0]
    key_rows = split[:, :, 1]
    values = split[:, :, 2]
    raw_scores = mixed('bqhd,bkhd->bhqk', queries, key_rows) * HD ** (-0.5)
    valid_keys = jnp.arange(SEQ).astype(jnp.int32)[None, :] < slot_lens[:, None]
    scores = jnp.where(valid_keys[:, None, None, :], low_back(raw_scores), -1e+30)
    row_max = lax.optimization_barrier(jnp.max(scores, axis=-1, keepdims=True))
    exp_scores = jnp.exp(scores - row_max)
    soft_weights = exp_scores / lax.optimization_barrier(jnp.sum(exp_scores, axis=-1, keepdims=True))
    context = mixed('bhqk,bkhd->bqhd', low(soft_weights), values).reshape(batch, SEQ, D)
    context = low(low_back(context))
    attn_out = low_back(mixed('bsd,de->bse', context, out_weight) + out_bias)
    hidden = layer_norm(row_data + attn_out, attn_gain, attn_shift)
    pre_act = low_back(mixed('bsd,df->bsf', low(hidden), up_weight) + up_bias)
    activ = low(gelu_exact(pre_act))
    down_out = low_back(mixed('bsf,fd->bsd', activ, down_weight) + down_bias)
    normed = layer_norm(hidden + down_out, mlp_gain, mlp_shift)
    return normed * valid_keys[:, :, None].astype(jnp.float32)

def reference(tokens, lengths, slot_order, qkv_weight, qv_bias, out_weight, out_bias, attn_gain, attn_shift, up_weight, up_bias, down_weight, down_bias, mlp_gain, mlp_shift, cotangent):
    slot_lens = lengths[slot_order.astype(jnp.int32)].astype(jnp.int32)
    params = tuple((item.astype(jnp.float32) for item in (qkv_weight, qv_bias, out_weight, out_bias, attn_gain, attn_shift, up_weight, up_bias, down_weight, down_bias, mlp_gain, mlp_shift)))
    group_count = NSEQ // 8
    lens_grouped = slot_lens.reshape(group_count, 8)

    def forward(weights_all, row_data):
        grouped = row_data.reshape(group_count, 8, SEQ, D)
        step_fn = jax.checkpoint(partial(block_forward, weights_all))

        def scan_step(carry, item):
            return (carry, step_fn(item[0], item[1]))
        unused, outputs = lax.scan(scan_step, jnp.zeros((), jnp.float32), (grouped, lens_grouped))
        return outputs.reshape(NSEQ, SEQ, D)
    layer_out, pullback = jax.vjp(forward, params, tokens.astype(jnp.float32))
    grad_params, grad_rows = pullback(cotangent.astype(jnp.float32))
    return (layer_out.astype(jnp.bfloat16), grad_rows.astype(jnp.bfloat16), grad_params[0], grad_params[1], grad_params[2], grad_params[3], grad_params[4], grad_params[5], grad_params[6], grad_params[7], grad_params[8], grad_params[9], grad_params[10], grad_params[11])
```

```python
import jax
import jax.numpy as jnp
from jax import lax
from jax.experimental import pallas as pl
from jax.experimental.pallas import tpu as pltpu
from jax.sharding import Mesh
from jax.sharding import PartitionSpec as P

HEADS = 12
LANES = 128
NT = (((1,), (1,)), ((), ()))
NN = (((1,), (0,)), ((), ()))
TN = (((0,), (0,)), ((), ()))


def dot(left, right, dims):
    return lax.dot_general(left, right, dims, preferred_element_type=jnp.float32)


def layer_norm(row_data, gain_row, shift_row):
    row_mean = jnp.mean(row_data, axis=-1, keepdims=True)
    centred = row_data - row_mean
    spread = jnp.mean(centred * centred, axis=-1, keepdims=True)
    return centred * lax.rsqrt(spread + 1e-06) * gain_row + shift_row


def gelu_exact(values):
    return 0.5 * values * (1.0 + lax.erf(values * 0.7071067811865476))


def column_sum(grad_rows):
    return jnp.sum(grad_rows.astype(jnp.float32), axis=0)


def attend_kernel(lens_ref, qkv_ref, ctx_ref, lse_ref, *, width, head_size):
    seqlen = qkv_ref.shape[0]
    valid = lax.broadcasted_iota(jnp.int32, (seqlen, seqlen), 0) < lens_ref[pl.program_id(0)]
    scale = head_size ** (-0.5)
    per = LANES // head_size
    for pair in range(width // LANES):
        at = pair * LANES
        queries = qkv_ref[:, at : at + LANES] * jnp.asarray(scale, jnp.bfloat16)
        key_rows = qkv_ref[:, width + at : width + at + LANES]
        values = qkv_ref[:, 2 * width + at : 2 * width + at + LANES]
        parts = []
        for sub in range(per):
            cut = slice(sub * head_size, (sub + 1) * head_size)
            scores = dot(key_rows[:, cut], queries[:, cut], NT)
            scores = jnp.where(valid, scores, -1e30)
            top = jnp.max(scores, axis=0, keepdims=True)
            grown = jnp.exp(scores - top)
            total = jnp.sum(grown, axis=0, keepdims=True)
            soft = (grown * (1.0 / total)).astype(jnp.bfloat16)
            parts.append(dot(soft, values[:, cut], TN))
            lse_ref[0, pair * per + sub : pair * per + sub + 1, :] = top + jnp.log(total)
        ctx_ref[:, at : at + LANES] = jnp.concatenate(parts, axis=1).astype(jnp.bfloat16)


def attend_back_kernel(lens_ref, qkv_ref, lse_ref, dctx_ref, dqkv_ref, *, width, head_size):
    seqlen = qkv_ref.shape[0]
    valid = lax.broadcasted_iota(jnp.int32, (seqlen, seqlen), 0) < lens_ref[pl.program_id(0)]
    scale = head_size ** (-0.5)
    per = LANES // head_size
    for pair in range(width // LANES):
        at = pair * LANES
        queries = qkv_ref[:, at : at + LANES] * jnp.asarray(scale, jnp.bfloat16)
        key_rows = qkv_ref[:, width + at : width + at + LANES]
        values = qkv_ref[:, 2 * width + at : 2 * width + at + LANES]
        dctx = dctx_ref[:, at : at + LANES]
        dq, dk, dv = [], [], []
        for sub in range(per):
            cut = slice(sub * head_size, (sub + 1) * head_size)
            scores = dot(key_rows[:, cut], queries[:, cut], NT)
            lse = lse_ref[0, pair * per + sub : pair * per + sub + 1, :]
            soft = jnp.where(valid, jnp.exp(scores - lse), 0.0)
            dsoft = dot(values[:, cut], dctx[:, cut], NT)
            dv.append(dot(soft.astype(jnp.bfloat16), dctx[:, cut], NN))
            inner = jnp.sum(soft * dsoft, axis=0, keepdims=True)
            dscores = (soft * (dsoft - inner)).astype(jnp.bfloat16)
            dq.append(dot(dscores, key_rows[:, cut], TN) * scale)
            dk.append(dot(dscores, queries[:, cut], NN))
        for place, part in enumerate((dq, dk, dv)):
            start = place * width + at
            dqkv_ref[:, start : start + LANES] = jnp.concatenate(part, axis=1).astype(jnp.bfloat16)


def attend(slot_lens, projected, slot_count, head_count):
    rows, wide = projected.shape
    seqlen, width = rows // slot_count, wide // 3
    head_size = width // head_count
    return pl.pallas_call(
        lambda *refs: attend_kernel(*refs, width=width, head_size=head_size),
        grid_spec=pltpu.PrefetchScalarGridSpec(
            num_scalar_prefetch=1,
            grid=(slot_count,),
            in_specs=[pl.BlockSpec((seqlen, wide), lambda i, lens: (i, 0))],
            out_specs=[
                pl.BlockSpec((seqlen, width), lambda i, lens: (i, 0)),
                pl.BlockSpec((1, head_count, seqlen), lambda i, lens: (i, 0, 0)),
            ],
        ),
        out_shape=[
            jax.ShapeDtypeStruct((rows, width), jnp.bfloat16),
            jax.ShapeDtypeStruct((slot_count, head_count, seqlen), jnp.float32),
        ],
        compiler_params=pltpu.CompilerParams(vmem_limit_bytes=48 * 2**20),
        cost_estimate=pl.CostEstimate(
            flops=4 * rows * seqlen * width * 4,
            bytes_accessed=8 * rows * width,
            transcendentals=rows * seqlen * head_count,
        ),
        name="attend",
    )(slot_lens, projected)


def attend_back(slot_lens, projected, lse, dctx, slot_count, head_count):
    rows, wide = projected.shape
    seqlen, width = rows // slot_count, wide // 3
    head_size = width // head_count
    return pl.pallas_call(
        lambda *refs: attend_back_kernel(*refs, width=width, head_size=head_size),
        grid_spec=pltpu.PrefetchScalarGridSpec(
            num_scalar_prefetch=1,
            grid=(slot_count,),
            in_specs=[
                pl.BlockSpec((seqlen, wide), lambda i, lens: (i, 0)),
                pl.BlockSpec((1, head_count, seqlen), lambda i, lens: (i, 0, 0)),
                pl.BlockSpec((seqlen, width), lambda i, lens: (i, 0)),
            ],
            out_specs=pl.BlockSpec((seqlen, wide), lambda i, lens: (i, 0)),
        ),
        out_shape=jax.ShapeDtypeStruct((rows, wide), jnp.bfloat16),
        compiler_params=pltpu.CompilerParams(vmem_limit_bytes=48 * 2**20),
        cost_estimate=pl.CostEstimate(
            flops=10 * rows * seqlen * width * 4,
            bytes_accessed=14 * rows * width,
            transcendentals=rows * seqlen * head_count,
        ),
        name="attend_back",
    )(slot_lens, projected, lse, dctx)


def hop(part, axis, mask):
    pairs = [(place, place ^ mask) for place in range(lax.axis_size(axis))]
    return lax.ppermute(part, axis, pairs)


def take(parts, index):
    return lax.dynamic_index_in_dim(parts, index, 0, keepdims=False)


def add(left, right):
    return left.astype(jnp.float32) + right.astype(jnp.float32)


def low(part):
    return part.astype(jnp.bfloat16)


def gather_start(shard):
    rows, cols = shard.shape
    halves = shard.reshape(2, 2, rows // 4, cols)
    mine = take(halves, lax.axis_index("core"))
    first = hop(mine, "replica", 1)
    second = hop(mine, "replica", 2)
    return first, second


def gather_end(shard, first, second):
    rows, cols = shard.shape
    me, core = lax.axis_index("replica"), lax.axis_index("core")
    third = jnp.stack([hop(first[0], "replica", 2), hop(second[1], "replica", 1)])
    halves = shard.reshape(2, 2, rows // 4, cols)
    mine = [first, second, third]
    theirs = [hop(part, "core", 1) for part in mine]
    blocks = [halves]
    for own, other in zip(mine, theirs):
        low_half = jnp.where(core == 0, own, other)
        high_half = jnp.where(core == 0, other, own)
        blocks.append(jnp.stack([low_half, high_half]))
    full = jnp.stack(blocks)
    return jnp.concatenate([take(full, me ^ owner) for owner in range(4)], axis=0).reshape(
        4 * rows, cols
    )


def gather_small(row):
    me = lax.axis_index("replica")
    near = jnp.stack([row, hop(row, "replica", 1)])
    full = jnp.concatenate([near, hop(near, "replica", 2)], axis=0)
    return jnp.stack([take(full, me ^ owner) for owner in range(4)])


def sum_small(rows):
    for axis in ("core", "replica", "chain"):
        mask = 1
        while mask < lax.axis_size(axis):
            rows = rows + hop(rows, axis, mask)
            mask *= 2
    return rows


def share(grad):
    rows, cols = grad.shape
    me, core = lax.axis_index("replica"), lax.axis_index("core")
    place, depth = lax.axis_index("chain"), lax.axis_size("chain")
    pieces = low(grad).reshape(4, 2, 2, rows // 16, cols)
    own = lax.dynamic_index_in_dim(pieces, core, 1, keepdims=False)
    other = lax.dynamic_index_in_dim(pieces, 1 - core, 1, keepdims=False)
    part = low(add(own, hop(other, "core", 1)))
    front, back = part[:, 0], part[:, 1]
    got_front = hop(jnp.stack([take(front, me ^ 1), take(front, me ^ 3)]), "replica", 1)
    got_back = hop(jnp.stack([take(back, me ^ 2), take(back, me ^ 3)]), "replica", 2)
    far_front = hop(low(add(take(front, me ^ 2), got_front[1])), "replica", 2)
    far_back = hop(low(add(take(back, me ^ 1), got_back[1])), "replica", 1)
    total = jnp.concatenate(
        [
            add(add(take(front, me), got_front[0]), far_front),
            add(add(take(back, me), got_back[0]), far_back),
        ],
        axis=0,
    )
    total = low(total)
    mask = 1
    while mask < depth:
        bit = (place // mask) % 2
        split = total.reshape(2, total.shape[0] // 2, cols)
        total = low(add(take(split, bit), hop(take(split, 1 - bit), "chain", mask)))
        mask *= 2
    while mask > 1:
        mask //= 2
        bit = (place // mask) % 2
        other = hop(total, "chain", mask)
        total = jnp.concatenate(
            [jnp.where(bit == 0, total, other), jnp.where(bit == 0, other, total)], axis=0
        )
    other = hop(total, "core", 1)
    return jnp.concatenate(
        [jnp.where(core == 0, total, other), jnp.where(core == 0, other, total)], axis=0
    ).astype(jnp.float32)


def body(
    tokens,
    lengths,
    slot_order,
    qkv_weight,
    qv_bias,
    out_weight,
    out_bias,
    attn_gain,
    attn_shift,
    up_weight,
    up_bias,
    down_weight,
    down_bias,
    mlp_gain,
    mlp_shift,
    cotangent,
):
    slot_count, seqlen, width = tokens.shape
    row_count = slot_count * seqlen
    owners = lax.axis_size("replica")
    picked = slot_order[:, None] == jnp.arange(lengths.shape[0], dtype=jnp.int32)[None, :]
    slot_lens = jnp.sum(jnp.where(picked, lengths[None, :], 0), axis=1)
    valid_rows = jnp.arange(seqlen, dtype=jnp.int32)[None, :] < slot_lens[:, None]
    row_valid = valid_rows.reshape(row_count, 1).astype(jnp.float32)

    small = (qv_bias, out_bias, attn_gain, attn_shift, up_bias, down_bias, mlp_gain, mlp_shift)
    sizes = [part.shape[0] for part in small]
    packed = gather_small(jnp.concatenate(small))
    full_small, at = [], 0
    for size in sizes:
        full_small.append(packed[:, at : at + size].reshape(owners * size).astype(jnp.float32))
        at += size
    qv, outb, gain1, shift1, upb, downb, gain2, shift2 = full_small
    first, second = gather_start(qkv_weight)
    full_qkv = gather_end(qkv_weight, first, second)
    first, out_shard, up_shard, down_shard = lax.optimization_barrier(
        (first, out_weight, up_weight, down_weight)
    )
    full_out = gather_end(out_shard, *gather_start(out_shard))
    full_up = gather_end(up_shard, *gather_start(up_shard))
    full_down = gather_end(down_shard, *gather_start(down_shard))

    flat = tokens.reshape(row_count, width)
    bias_row = jnp.concatenate([qv[:width], jnp.zeros((width,), jnp.float32), qv[width:]])
    projected = (dot(flat, full_qkv, NN) + bias_row).astype(jnp.bfloat16)
    ctx, lse = attend(slot_lens, projected, slot_count, HEADS)
    res1 = flat.astype(jnp.float32) + dot(ctx, full_out, NN) + outb
    hidden = layer_norm(res1, gain1, shift1)
    hidden_low = hidden.astype(jnp.bfloat16)
    pre_act = dot(hidden_low, full_up, NN) + upb
    activ_low = gelu_exact(pre_act).astype(jnp.bfloat16)
    res2 = hidden + dot(activ_low, full_down, NN) + downb
    normed = layer_norm(res2, gain2, shift2)
    layer_out = (normed * row_valid).astype(jnp.bfloat16).reshape(slot_count, seqlen, width)

    grad_out = cotangent.reshape(row_count, width).astype(jnp.float32) * row_valid
    unused_second, second_pull = jax.vjp(layer_norm, res2, gain2, shift2)
    dres2, grad_gain2, grad_shift2 = second_pull(grad_out)
    ddown = dres2.astype(jnp.bfloat16)
    grad_down = share(dot(activ_low, ddown, TN))
    dactiv = dot(ddown, full_down, NT)
    unused_act, gelu_pull = jax.vjp(gelu_exact, pre_act)
    dpre = gelu_pull(dactiv)[0].astype(jnp.bfloat16)
    grad_up = share(dot(hidden_low, dpre, TN))
    dhidden = dres2 + dot(dpre, full_up, NT)
    unused_first, first_pull = jax.vjp(layer_norm, res1, gain1, shift1)
    dres1, grad_gain1, grad_shift1 = first_pull(dhidden)
    dattn = dres1.astype(jnp.bfloat16)
    grad_out_weight = share(dot(ctx, dattn, TN))
    dctx = dot(dattn, full_out, NT).astype(jnp.bfloat16)
    dqkv = attend_back(slot_lens, projected, lse, dctx, slot_count, HEADS)
    grad_qkv = share(dot(flat, dqkv, TN))
    proj_sums = column_sum(dqkv)
    grad_tokens = (dres1 + dot(dqkv, full_qkv, NT)).astype(jnp.bfloat16)
    grad_tokens = grad_tokens.reshape(slot_count, seqlen, width)

    small_grads = (
        jnp.concatenate([proj_sums[:width], proj_sums[2 * width :]]),
        column_sum(dattn),
        grad_gain1,
        grad_shift1,
        column_sum(dpre),
        column_sum(ddown),
        grad_gain2,
        grad_shift2,
    )
    together = jnp.concatenate([part.reshape(owners, -1) for part in small_grads], axis=1)
    summed = sum_small(together)
    own = lax.dynamic_slice_in_dim(summed, lax.axis_index("replica"), 1, 0)[0]
    shares, at = [], 0
    for size in sizes:
        shares.append(own[at : at + size])
        at += size
    return (
        layer_out,
        grad_tokens,
        grad_qkv,
        shares[0],
        grad_out_weight,
        shares[1],
        shares[2],
        shares[3],
        grad_up,
        shares[4],
        grad_down,
        shares[5],
        shares[6],
        shares[7],
    )


def solution(mesh):
    owners, sharers = mesh.devices.shape
    split = Mesh(mesh.devices.reshape(owners, sharers // 2, 2), ("replica", "chain", "core"))
    rows = P(("replica", "chain", "core"), None, None)
    flat = P("replica")
    wide = P("replica", None)
    weights = (wide, flat, wide, flat, flat, flat, wide, flat, wide, flat, flat, flat)
    return jax.shard_map(
        body,
        mesh=split,
        in_specs=(rows, P(), P(("replica", "chain", "core"))) + weights + (rows,),
        out_specs=(rows, rows) + weights,
        check_vma=False,
    )
```
